256 devices in a mesh: seq: 32 (over z_hi, y, core), head: 8 (over z_lo, x).
Axes of the slice: x: 4, y: 4, z: 8 (z_hi: 4, z_lo: 2; z = z_hi * 2 + z_lo), core: 2. Of those that a mesh axis runs over, the one named last changes fastest.
Arguments:
- queries: bfloat16 [32768, 6144], P(('seq', 'head')), may hold values from -8 to 8
- keys: bfloat16 [32768, 6144], P(('seq', 'head')), may hold values from -8 to 8
- values: bfloat16 [32768, 6144], P(('seq', 'head')), may hold values from -15 to 15
- block_lists: int32 [256, 20], P('seq'), may hold values from 0 to 255, as said below
- live_counts: int32 [256], P('seq'), may hold values from 10 to 20, as said below
Outputs:
- attended: bfloat16 [32768, 6144], P(('seq', 'head'))
The draws below stay inside these ranges and needn't reach their ends.
Inputs may be any that keep to these rules, and one draw needn't show every extreme that they name: `block_lists`: slot 0 of row b is b itself; a row's blocks are distinct. With the band of block g being g // 8 and its place p = g % 8, a query block of band t names only blocks of bands t - 2 to t + 2 taken modulo the number of bands; of band t - 2 only places p >= 4, of band t + 2 only places p < 4. `live_counts`: the first query block of every latitude band has 20.
All inputs are finite; a program needn't handle non-finite values.
Results may differ from the reference program's by a relative error of at most 0.0037.
Values may be sent and summed in bfloat16 or wider, within the bound.
A program may use at most 128 MiB of HBM per device.

```python
import jax
import jax.numpy as jnp
from jax import lax

HEADS = 48
HD = 128
BLK = 128
KB = 20
QB_DEV = 8
TOKENS = 32768
QBLOCKS = 256


def draw_queries(key, part):
    key = jax.random.fold_in(key, 1)
    result = 1.4 * jax.random.truncated_normal(key, -5.5, 5.5, (TOKENS, HEADS * HD), jnp.float32)
    return result.astype(jnp.bfloat16)


def draw_keys(key, part):
    key = jax.random.fold_in(key, 2)
    result = 1.4 * jax.random.truncated_normal(key, -5.5, 5.5, (TOKENS, HEADS * HD), jnp.float32)
    return result.astype(jnp.bfloat16)


def draw_block_lists(key, part):
    key = jax.random.fold_in(key, 5)
    half_band = QB_DEV // 2
    cand_offset = jnp.concatenate([jnp.full((half_band,), -2), jnp.full((QB_DEV,), -1), jnp.zeros((QB_DEV,)), jnp.full((QB_DEV,), 1), jnp.full((half_band,), 2)]).astype(jnp.int32)
    cand_place = jnp.concatenate([jnp.arange(half_band, QB_DEV), jnp.arange(QB_DEV), jnp.arange(QB_DEV), jnp.arange(QB_DEV), jnp.arange(half_band)]).astype(jnp.int32)
    block_ids = jnp.arange(QBLOCKS, dtype=jnp.int32)
    band_ids = block_ids // QB_DEV
    own_slot = half_band + QB_DEV + block_ids % QB_DEV
    row_keys = jax.random.split(key, QBLOCKS)
    orders = jax.vmap(lambda row_key: jax.random.permutation(row_key, 4 * QB_DEV - 1))(row_keys)
    chosen = orders[:, :KB - 1].astype(jnp.int32)
    chosen = chosen + (chosen >= own_slot[:, None]).astype(jnp.int32)
    band_count = QBLOCKS // QB_DEV
    target = (band_ids[:, None] + cand_offset[chosen]) % band_count * QB_DEV + cand_place[chosen]
    return jnp.concatenate([block_ids[:, None], target], axis=1).astype(jnp.int32)


def draw_live_counts(key, part):
    key = jax.random.fold_in(key, 3)
    counts = jax.random.randint(key, (QBLOCKS,), KB // 2, KB + 1)
    first_block = jnp.arange(QBLOCKS, dtype=jnp.int32) % QB_DEV == 0
    return jnp.where(first_block, KB, counts).astype(jnp.int32)


def shard_levels(own_key, shape, cuts, smallest, largest):
    def one(position, blocks):
        heights = jax.random.uniform(jax.random.fold_in(jax.random.fold_in(own_key, 6), position), (blocks,), jnp.float32, smallest / len(cuts), largest / len(cuts))
        return jnp.repeat(jnp.exp(heights), shape[position] // blocks).reshape((-1,) + (1,) * (len(shape) - position - 1))

    loudness = one(*cuts[0])
    for cut in cuts[1:]:
        loudness = loudness * one(*cut)
    return loudness


def scatter_about(rng, dims, deviation, most, cuts=(), kind=jnp.bfloat16):
    values = deviation * jax.random.normal(rng, dims, jnp.float32)
    if cuts:
        values = values * shard_levels(rng, dims, cuts, -0.22, 0.18)
    return jnp.clip(values, -most, most).astype(kind)


def setup_inputs(seed: int = 0) -> dict:
    key_list = jax.random.split(jax.random.key(seed), 6)
    return {
        "queries": draw_queries(jax.random.fold_in(key_list[5], 71), 0),
        "keys": draw_keys(jax.random.fold_in(key_list[5], 71), 0),
        "values": scatter_about(key_list[2], (TOKENS, HEADS * HD), 3.0, 15.0, ((0, 256),)),
        "block_lists": draw_block_lists(jax.random.fold_in(key_list[5], 71), 0),
        "live_counts": draw_live_counts(jax.random.fold_in(key_list[5], 71), 0),
    }


def attend_block(query_rows, key_rows, value_rows, live_count, head_count, head_size):
    block_rows = query_rows.shape[0]
    query_heads = query_rows.astype(jnp.float32).reshape(block_rows, head_count, head_size)
    key_heads = key_rows.astype(jnp.float32).reshape(-1, head_count, head_size)
    value_heads = value_rows.astype(jnp.float32).reshape(-1, head_count, head_size)
    scores = jnp.einsum("qhd,khd->hqk", query_heads, key_heads) * (head_size ** -0.5)
    is_valid = (jnp.arange(key_heads.shape[0], dtype=jnp.int32) // block_rows) < live_count
    scores = jnp.where(is_valid[None, None, :], scores, jnp.float32(-1e30))
    row_max = jnp.max(scores, axis=-1, keepdims=True)
    expo = jnp.where(is_valid[None, None, :], jnp.exp(scores - row_max), jnp.float32(0.0))
    row_total = jnp.sum(expo, axis=-1)
    weights = lax.optimization_barrier(expo.astype(jnp.bfloat16)).astype(jnp.float32)
    summed = jnp.einsum("hqk,khd->qhd", weights, value_heads)
    result = summed / jnp.transpose(row_total)[:, :, None]
    return result.reshape(block_rows, head_count * head_size).astype(jnp.bfloat16)


def reference(queries, keys, values, block_lists, live_counts):
    width_all = HEADS * HD
    key_blocks = keys.reshape(QBLOCKS, BLK, width_all)
    value_blocks = values.reshape(QBLOCKS, BLK, width_all)

    def one_block(block_index):
        query_rows = lax.dynamic_slice_in_dim(queries, block_index * BLK, BLK, 0)
        chosen = block_lists[block_index]
        key_rows = key_blocks[chosen].reshape(KB * BLK, width_all)
        value_rows = value_blocks[chosen].reshape(KB * BLK, width_all)
        return attend_block(query_rows, key_rows, value_rows, live_counts[block_index], HEADS, HD)

    result = lax.map(one_block, jnp.arange(QBLOCKS, dtype=jnp.int32))
    return result.reshape(TOKENS, width_all)
```

```python
import functools
import math

import jax
import jax.numpy as jnp
from jax import lax
from jax.experimental import pallas as pl
from jax.experimental.pallas import tpu as pltpu
from jax.sharding import PartitionSpec as P

HD = 128
BLK = 128
KB = 20
SB = 16
HALO = 12
WIN = HALO + SB + HALO
PH = 3
UNROLL = 4
LANES = 128
MESH = pl.DeviceIdType.MESH
EXP2_SCALE = math.log2(math.e) / math.sqrt(HD)


def xor_bit(a, b):
    return a + b - 2 * a * b


def member_device(band, slot):
    y_hi = (band // 2) % 2
    y_lo = xor_bit(slot // 8, y_hi)
    return (band // 4) * 8 + (y_hi * 2 + y_lo) * 2 + band % 2, slot % 8


def attend(block, q_ref, k_ref, v_ref, ones_ref, lists, s_ref):
    query = q_ref[block]
    top = None
    for c in range(KB // 2):
        picked = [k_ref[lists[block, 2 * c + t]] for t in range(2)]
        scores = lax.dot_general(
            query, jnp.concatenate(picked, axis=0), (((1,), (1,)), ((), ())),
            preferred_element_type=jnp.float32,
        )
        s_ref[c] = scores
        top = scores if top is None else jnp.maximum(top, scores)
    top = jnp.max(top, axis=1, keepdims=True) * EXP2_SCALE
    total = None
    for c in range(KB // 2):
        weights = jnp.exp2(s_ref[c] * EXP2_SCALE - top).astype(jnp.bfloat16)
        picked = [
            jnp.concatenate(
                [v_ref[lists[block, 32 + 2 * c + t]], ones_ref[lists[block, 64 + 2 * c + t]]], axis=1
            )
            for t in range(2)
        ]
        part = jnp.dot(weights, jnp.concatenate(picked, axis=0), preferred_element_type=jnp.float32)
        total = part if total is None else total + part
    return (total[:, :HD] / total[:, HD:]).astype(jnp.bfloat16)


def kernel(*refs):
    q_in, k_in, v_in, lists_in, out = refs[:5]
    q, k, v = refs[5:8], refs[8:11], refs[11:14]
    ones_ref, staged, lists_v, lists_s = refs[14:18]
    scores = refs[18 : 18 + UNROLL]
    (q_send, k_send, v_send, l_send, q_recv, k_recv, v_recv, l_recv, l_sem,
     kf_send, vf_send, kf_recv, vf_recv, o_send, o_recv) = refs[18 + UNROLL :]

    seq, head = lax.axis_index("seq"), lax.axis_index("head")
    bands = lax.axis_size("seq") // 2
    y_hi, y_lo, core = (seq // 4) % 2, (seq // 2) % 2, seq % 2
    half = xor_bit(y_lo, y_hi)
    my_band = (seq // 8) * 4 + y_hi * 2 + core
    my_slot = half * 8 + head
    own_band = seq // 2
    own_block = core * 8 + head
    to_self = own_band == my_band
    neighbours = {
        side: member_device((my_band + side + bands) % bands, my_slot) for side in (-1, 1)
    }

    ones_ref[0] = jnp.ones((BLK, HD), jnp.bfloat16)
    ones_ref[1] = jnp.zeros((BLK, HD), jnp.bfloat16)
    for h in range(PH):
        v[h][WIN] = jnp.zeros((BLK, HD), jnp.bfloat16)

    bits = [own_block % 2, (own_block // 2) % 2, (own_block // 4) % 2, own_block // 8]

    def slot_at(step):
        return sum(
            (1 - bit if step >> b & 1 else bit) * (1 << b) for b, bit in enumerate(bits)
        )

    barrier = pltpu.get_barrier_semaphore()

    def greet(device):
        pl.semaphore_signal(barrier, inc=1, device_id=device, device_id_type=MESH)

    def not_me(device):
        return jnp.logical_or(device[0] != seq, device[1] != head)

    for side in (-1, 1):
        greet(neighbours[side])
    for n in range(SB):
        for device in (
            member_device(own_band, slot_at(n)),
            (2 * my_band + n // 8, jnp.int32(n % 8)),
        ):
            pl.when(not_me(device))(functools.partial(greet, device))

    @pl.when(to_self)
    def _():
        pl.semaphore_wait(barrier, 2 * SB)

    @pl.when(jnp.logical_not(to_self))
    def _():
        pl.semaphore_wait(barrier, 2 * SB + 2)

    def push(src, dst, send, recv, device):
        @pl.when(not_me(device))
        def _():
            pltpu.make_async_remote_copy(
                src_ref=src, dst_ref=dst, send_sem=send, recv_sem=recv,
                device_id=device, device_id_type=MESH,
            ).start()

        @pl.when(jnp.logical_not(not_me(device)))
        def _():
            pltpu.make_async_copy(src, dst, recv).start()

    def columns(slot, h):
        return pl.ds(pl.multiple_of((slot * PH + h) * HD, HD), HD)

    def scatter_lists():
        for n in (0, 8):
            push(lists_in, lists_v.at[pl.ds(pl.multiple_of(core * 8, 8), 8)], l_send,
                 l_recv.at[core], member_device(own_band, slot_at(n)))

    def scatter(h):
        for n in range(SB):
            slot = slot_at(n)
            device = member_device(own_band, slot)
            cols, group = columns(slot, h), own_block // 4
            push(k_in.at[:, cols], k[h].at[HALO + own_block], k_send, k_recv.at[h, group], device)
            push(v_in.at[:, cols], v[h].at[HALO + own_block], v_send, v_recv.at[h, group], device)
        for n in range(SB):
            slot = slot_at(n)
            device = member_device(own_band, slot)
            push(q_in.at[:, columns(slot, h)], q[h].at[own_block], q_send, q_recv.at[h], device)

    def arrived(ref, sem):
        pltpu.make_async_copy(ref, ref, sem).wait()

    def forward(h, step):
        group = 2 * xor_bit(half, step // 2) + xor_bit(head // 4, step % 2)
        own = pl.ds(HALO + group * 4, 4)
        for buf, own_sem, send, recv in (
            (k[h], k_recv, kf_send, kf_recv), (v[h], v_recv, vf_send, vf_recv)
        ):
            arrived(buf.at[own], own_sem.at[h, group])

            @pl.when(group >= 1)
            def _():
                pltpu.make_async_remote_copy(
                    src_ref=buf.at[own], dst_ref=buf.at[pl.ds(group * 4 - 4, 4)],
                    send_sem=send.at[h], recv_sem=recv.at[h, 0],
                    device_id=neighbours[1], device_id_type=MESH,
                ).start()

            @pl.when(group <= 2)
            def _():
                pltpu.make_async_remote_copy(
                    src_ref=buf.at[own], dst_ref=buf.at[pl.ds(HALO + SB + group * 4, 4)],
                    send_sem=send.at[h], recv_sem=recv.at[h, 1],
                    device_id=neighbours[-1], device_id_type=MESH,
                ).start()

    scatter_lists()
    scatter(0)
    scatter(1)
    for band in range(2):
        arrived(lists_v.at[pl.ds(band * 8, 8)], l_recv.at[band])
    move = pltpu.make_async_copy(lists_v, lists_s, l_sem)
    move.start()
    move.wait()
    for step in range(4):
        forward(0, step)
    scatter(2)

    for h in range(PH):
        arrived(q[h], q_recv.at[h])
        for side, start in ((0, 0), (1, HALO + SB)):
            arrived(k[h].at[pl.ds(start, HALO)], kf_recv.at[h, side])
            arrived(v[h].at[pl.ds(start, HALO)], vf_recv.at[h, side])

        @pl.loop(0, SB // UNROLL)
        def _(step):
            if h + 1 < PH:
                forward(h + 1, step)
            for u in range(UNROLL):
                block = step * UNROLL + u
                staged[h, block] = attend(block, q[h], k[h], v[h], ones_ref, lists_s, scores[u])
            for u in range(UNROLL):
                block = step * UNROLL + u
                push(staged.at[h, block], out.at[:, columns(my_slot, h)], o_send, o_recv,
                     (2 * my_band + block // 8, block % 8))

    arrived(out, o_recv)
    sent = (
        (k_in, k_send), (v_in, v_send), (q_in, q_send),
    )

    @pl.when(to_self)
    def _():
        some = pl.ds(0, (SB - 1) * PH * HD)
        for ref, sem in sent:
            arrived(ref.at[:, some], sem)
        arrived(staged.at[:, pl.ds(0, SB - 1)], o_send)
        arrived(lists_v.at[pl.ds(0, 8)], l_send)

    @pl.when(jnp.logical_not(to_self))
    def _():
        for ref, sem in sent:
            arrived(ref, sem)
        arrived(staged, o_send)
        arrived(lists_v, l_send)

    for h in range(PH):
        arrived(k[h].at[pl.ds(0, 2 * HALO)], kf_send.at[h])
        arrived(v[h].at[pl.ds(0, 2 * HALO)], vf_send.at[h])


def local(queries, keys, values, block_lists, live_counts):
    seq = lax.axis_index("seq")
    blocks = lax.axis_size("seq") * block_lists.shape[0]
    window = jnp.remainder(block_lists - (seq // 2) * SB + HALO, blocks)
    live = jnp.arange(KB, dtype=jnp.int32)[None, :] < live_counts[:, None]
    k_index = jnp.where(live, window, window[:, :1])
    v_index = jnp.where(live, window, WIN)
    dead = jnp.where(live, 0, 1)
    pad = jnp.zeros((block_lists.shape[0], 32 - KB), jnp.int32)
    lists = jnp.concatenate([k_index, pad, v_index, pad, dead], axis=1)
    lists = jnp.pad(lists, ((0, 0), (0, LANES - lists.shape[1])))
    hbm = pl.BlockSpec(memory_space=pl.ANY)
    dma = pltpu.SemaphoreType.DMA
    bf16 = jnp.bfloat16
    return pl.pallas_call(
        kernel,
        out_shape=jax.ShapeDtypeStruct(queries.shape, bf16),
        in_specs=[hbm] * 4,
        out_specs=hbm,
        scratch_shapes=[pltpu.VMEM((SB, BLK, HD), bf16)] * PH
        + [pltpu.VMEM((WIN, BLK, HD), bf16)] * PH
        + [pltpu.VMEM((WIN + 1, BLK, HD), bf16)] * PH
        + [
            pltpu.VMEM((2, BLK, HD), bf16),
            pltpu.VMEM((PH, SB, BLK, HD), bf16),
            pltpu.VMEM((SB, LANES), jnp.int32),
            pltpu.SMEM((SB, LANES), jnp.int32),
        ]
        + [pltpu.VMEM((KB // 2, BLK, 2 * BLK), jnp.float32)] * UNROLL
        + [dma, dma, dma, dma]
        + [dma((PH,)), dma((PH, 4)), dma((PH, 4)), dma((2,)), dma]
        + [dma((PH,)), dma((PH,)), dma((PH, 2)), dma((PH, 2)), dma, dma],
        compiler_params=pltpu.CompilerParams(
            collective_id=0, has_side_effects=True, vmem_limit_bytes=48 << 20
        ),
    )(queries, keys, values, lists)


def solution(mesh):
    in_specs = (
        P(("seq", "head"), None),
        P(("seq", "head"), None),
        P(("seq", "head"), None),
        P("seq", None),
        P("seq"),
    )
    out_specs = P(("seq", "head"), None)
    return jax.shard_map(local, mesh=mesh, in_specs=in_specs, out_specs=out_specs, check_vma=False)
```

```python
import functools
import math

import jax
import jax.numpy as jnp
from jax import lax
from jax.experimental import pallas as pl
from jax.experimental.pallas import tpu as pltpu
from jax.sharding import PartitionSpec as P

HD = 128
BLK = 128
KB = 20
SB = 16
HALO = 12
WIN = HALO + SB + HALO
PH = 3
UNROLL = 4
LANES = 128
MESH = pl.DeviceIdType.MESH
EXP2_SCALE = math.log2(math.e) / math.sqrt(HD)


def xor_bit(a, b):
    return a + b - 2 * a * b


def device_at(x, y, z, core):
    return (z // 2) * 8 + y * 2 + core, (z % 2) * 4 + x


def attend(block, q_ref, k_ref, v_ref, ones_ref, lists, s_ref):
    query = q_ref[block]
    top = None
    for c in range(KB // 2):
        picked = [k_ref[lists[block, 2 * c + t]] for t in range(2)]
        scores = lax.dot_general(
            query, jnp.concatenate(picked, axis=0), (((1,), (1,)), ((), ())),
            preferred_element_type=jnp.float32,
        )
        s_ref[c] = scores
        top = scores if top is None else jnp.maximum(top, scores)
    top = jnp.max(top, axis=1, keepdims=True) * EXP2_SCALE
    total = None
    for c in range(KB // 2):
        weights = jnp.exp2(s_ref[c] * EXP2_SCALE - top).astype(jnp.bfloat16)
        picked = [
            jnp.concatenate(
                [v_ref[lists[block, 32 + 2 * c + t]], ones_ref[lists[block, 64 + 2 * c + t]]], axis=1
            )
            for t in range(2)
        ]
        part = jnp.dot(weights, jnp.concatenate(picked, axis=0), preferred_element_type=jnp.float32)
        total = part if total is None else total + part
    return (total[:, :HD] / total[:, HD:]).astype(jnp.bfloat16)


def kernel(*refs):
    q_in, k_in, v_in, lists_in, out = refs[:5]
    q, k, v = refs[5:8], refs[8:11], refs[11:14]
    q_pass, k_pass, v_pass = refs[14:17], refs[17:20], refs[20:23]
    ones_ref, staged, lists_v, lists_s = refs[23:27]
    scores = refs[27 : 27 + UNROLL]
    (q_send, k_send, v_send, l_send, q_recv, k_recv, v_recv, l_recv, l_sem,
     qp_recv, kp_recv, vp_recv, qf_send, kf_send, vf_send, kf_recv, vf_recv,
     o_send, o_recv) = refs[27 + UNROLL :]

    seq, head = lax.axis_index("seq"), lax.axis_index("head")
    planes = lax.axis_size("seq") // 4
    y, core, z_lo, x = (seq // 2) % 4, seq % 2, head // 4, head % 4
    z = (seq // 8) * 2 + z_lo
    my_band = 2 * z + core
    my_slot = y * 4 + x
    native = y // 2 == z_lo
    own_core = y % 2
    on_core = own_core == core

    sibling = device_at(x, y, z, 1 - core)
    partner = device_at(x, y, z + 1 - 2 * z_lo, core)
    across = device_at(x, y, (z + 2 * core - 1 + planes) % planes, 1 - core)

    ones_ref[0] = jnp.ones((BLK, HD), jnp.bfloat16)
    ones_ref[1] = jnp.zeros((BLK, HD), jnp.bfloat16)
    for h in range(PH):
        v[h][WIN] = jnp.zeros((BLK, HD), jnp.bfloat16)

    bits = [x % 2, x // 2, y % 2, y // 2]

    def slot_at(step):
        flipped = [1 - bit if step >> b & 1 else bit for b, bit in enumerate(bits)]
        return flipped[0] + 2 * flipped[1], flipped[2] + 2 * flipped[3]

    barrier = pltpu.get_barrier_semaphore()

    def greet(device):
        pl.semaphore_signal(barrier, inc=1, device_id=device, device_id_type=MESH)

    def not_me(device):
        return jnp.logical_or(device[0] != seq, device[1] != head)

    for device in (sibling, partner, across):
        greet(device)
    for n in range(SB):
        for device in (
            device_at(n % 4, n // 4, z, own_core),
            device_at(n % 4, core + 2 * (n // 8), z, (n // 4) % 2),
        ):
            pl.when(not_me(device))(functools.partial(greet, device))
    for n in range(SB // 2):
        greet((2 * my_band + n // 4, (1 - z_lo) * 4 + n % 4))

    @pl.when(jnp.logical_not(native))
    def _():
        for n in range(SB):
            greet(device_at(n % 4, n // 4, z + 1 - 2 * z_lo, own_core))

    off_plane, off_core = xor_bit(y // 2, z_lo), xor_bit(own_core, core)
    pl.semaphore_wait(barrier, 2 * SB + SB // 2 + 1 + SB * off_plane + 2 * off_core)

    def start(src, dst, send, recv, device):
        pltpu.make_async_remote_copy(
            src_ref=src, dst_ref=dst, send_sem=send, recv_sem=recv,
            device_id=device, device_id_type=MESH,
        ).start()

    def push(src, dst, send, recv, device):
        @pl.when(not_me(device))
        def _():
            start(src, dst, send, recv, device)

        @pl.when(jnp.logical_not(not_me(device)))
        def _():
            pltpu.make_async_copy(src, dst, recv).start()

    def columns(slot, h):
        return pl.ds(pl.multiple_of((slot * PH + h) * HD, HD), HD)

    def scatter_lists():
        for n in (0, 4, 8, 12):
            tx, ty = slot_at(n)
            push(lists_in, lists_v.at[pl.ds(pl.multiple_of(core * 8, 8), 8)], l_send,
                 l_recv.at[core], device_at(tx, ty, z, own_core))

    def scatter(h):
        def send_all(names):
            @pl.when(native)
            def _():
                for n in range(SB):
                    tx, ty = slot_at(n)
                    for src, dst, _, send, recv, _, first in names:
                        push(src.at[:, columns(ty * 4 + tx, h)],
                             dst[h].at[first + core * 8 + z_lo * 4 + x], send,
                             recv.at[h, core * 2 + z_lo], device_at(tx, ty, z, own_core))

            @pl.when(jnp.logical_not(native))
            def _():
                for n in range(SB):
                    tx, ty = slot_at(n)
                    for src, _, dst, send, _, recv, _ in names:
                        push(src.at[:, columns(ty * 4 + tx, h)],
                             dst[h].at[core * 4 + x], send,
                             recv.at[h, core], device_at(tx, ty, z, own_core))

        send_all(((k_in, k, k_pass, k_send, k_recv, kp_recv, HALO),
                  (v_in, v, v_pass, v_send, v_recv, vp_recv, HALO)))
        send_all(((q_in, q, q_pass, q_send, q_recv, qp_recv, 0),))

    def arrived(ref, sem):
        pltpu.make_async_copy(ref, ref, sem).wait()

    def four(start_block):
        return pl.ds(start_block, 4)

    def relay(h, part):
        group = part * 2 + z_lo
        src = four(part * 4)
        for buf, passed, pass_recv, send, own_recv, recv in (
            (k[h], k_pass[h], kp_recv, kf_send, k_recv, kf_recv),
            (v[h], v_pass[h], vp_recv, vf_send, v_recv, vf_recv),
        ):
            arrived(passed.at[src], pass_recv.at[h, part])
            start(passed.at[src], buf.at[four(HALO + group * 4)], send.at[h],
                  own_recv.at[h, group], partner)

            @pl.when(jnp.logical_and(core == 1, z_lo == 1))
            def _():
                start(passed.at[src], buf.at[four(part * 8)], send.at[h], recv.at[h, 0], sibling)

            @pl.when(jnp.logical_and(core == 0, z_lo == 0))
            def _():
                start(passed.at[src], buf.at[four(HALO + SB + part * 8)], send.at[h],
                      recv.at[h, 1], sibling)
        arrived(q_pass[h].at[src], qp_recv.at[h, part])
        start(q_pass[h].at[src], q[h].at[four(group * 4)], qf_send.at[h],
              q_recv.at[h, group], partner)

    right = tuple(jnp.where(core == 0, a, b) for a, b in zip(sibling, across))
    left = tuple(jnp.where(core == 0, b, a) for a, b in zip(sibling, across))

    def share(h, which):
        for part in range(2):
            group = part * 2 + xor_bit(z_lo, which)
            own = four(HALO + group * 4)
            to_right = jnp.logical_and(
                group >= 1,
                jnp.logical_or(jnp.logical_or(core == 0, z_lo == 1), group == 2),
            )
            to_left = jnp.logical_and(
                group <= 2,
                jnp.logical_or(jnp.logical_or(core == 1, z_lo == 0), group == 1),
            )
            for buf, own_recv, send, recv in (
                (k[h], k_recv, kf_send, kf_recv), (v[h], v_recv, vf_send, vf_recv)
            ):
                arrived(buf.at[own], own_recv.at[h, group])

                @pl.when(to_right)
                def _():
                    start(buf.at[own], buf.at[four(group * 4 - 4)], send.at[h],
                          recv.at[h, 0], right)

                @pl.when(to_left)
                def _():
                    start(buf.at[own], buf.at[four(HALO + SB + group * 4)], send.at[h],
                          recv.at[h, 1], left)

    def forward(h, step):
        @pl.when(step < 2)
        def _():
            relay(h, step)

        @pl.when(step >= 2)
        def _():
            share(h, step - 2)

    pl.when(native)(scatter_lists)
    scatter(0)
    scatter(1)
    for band in range(2):
        arrived(lists_v.at[pl.ds(band * 8, 8)], l_recv.at[band])
    move = pltpu.make_async_copy(lists_v.at[pl.ds(0, SB)], lists_s, l_sem)
    move.start()
    move.wait()
    for step in range(2):
        relay(0, step)
    scatter(2)
    for step in range(2):
        share(0, step)

    for h in range(PH):
        for group in range(4):
            arrived(q[h].at[four(group * 4)], q_recv.at[h, group])
        for side, first in ((0, 0), (1, HALO + SB)):
            arrived(k[h].at[pl.ds(first, HALO)], kf_recv.at[h, side])
            arrived(v[h].at[pl.ds(first, HALO)], vf_recv.at[h, side])

        @pl.loop(0, SB // UNROLL)
        def _(step):
            if h + 1 < PH:
                forward(h + 1, step)
            for u in range(UNROLL):
                block = step * UNROLL + u
                staged[h, block] = attend(block, q[h], k[h], v[h], ones_ref, lists_s, scores[u])
            for u in range(UNROLL):
                block = step * UNROLL + u
                push(staged.at[h, block], out.at[:, columns(my_slot, h)], o_send, o_recv,
                     (2 * my_band + block // 8, block % 8))

    arrived(out, o_recv)
    sent = ((k_in, k_send), (v_in, v_send), (q_in, q_send))

    @pl.when(on_core)
    def _():
        for ref, sem in sent:
            arrived(ref.at[:, pl.ds(0, (SB - 1) * PH * HD)], sem)

    @pl.when(jnp.logical_not(on_core))
    def _():
        for ref, sem in sent:
            arrived(ref, sem)

    mine = jnp.logical_and(on_core, native)

    @pl.when(mine)
    def _():
        arrived(staged.at[:, pl.ds(0, SB - 1)], o_send)
        arrived(lists_v.at[pl.ds(0, 24)], l_send)

    @pl.when(jnp.logical_not(mine))
    def _():
        arrived(staged, o_send)

    @pl.when(jnp.logical_and(jnp.logical_not(on_core), native))
    def _():
        arrived(lists_v, l_send)

    @pl.when(core == z_lo)
    def _():
        for h in range(PH):
            arrived(k[h], kf_send.at[h])
            arrived(v[h].at[pl.ds(0, WIN)], vf_send.at[h])

    @pl.when(core != z_lo)
    def _():
        for h in range(PH):
            arrived(k[h].at[pl.ds(0, 2 * HALO)], kf_send.at[h])
            arrived(v[h].at[pl.ds(0, 2 * HALO)], vf_send.at[h])

    for h in range(PH):
        arrived(q_pass[h], qf_send.at[h])


def local(queries, keys, values, block_lists, live_counts):
    seq = lax.axis_index("seq")
    blocks = lax.axis_size("seq") * block_lists.shape[0]
    window = jnp.remainder(block_lists - (seq // 2) * SB + HALO, blocks)
    live = jnp.arange(KB, dtype=jnp.int32)[None, :] < live_counts[:, None]
    k_index = jnp.where(live, window, window[:, :1])
    v_index = jnp.where(live, window, WIN)
    dead = jnp.where(live, 0, 1)
    pad = jnp.zeros((block_lists.shape[0], 32 - KB), jnp.int32)
    lists = jnp.concatenate([k_index, pad, v_index, pad, dead], axis=1)
    lists = jnp.pad(lists, ((0, 0), (0, LANES - lists.shape[1])))
    hbm = pl.BlockSpec(memory_space=pl.ANY)
    dma = pltpu.SemaphoreType.DMA
    bf16 = jnp.bfloat16
    return pl.pallas_call(
        kernel,
        out_shape=jax.ShapeDtypeStruct(queries.shape, bf16),
        in_specs=[hbm] * 4,
        out_specs=hbm,
        scratch_shapes=[pltpu.VMEM((SB, BLK, HD), bf16)] * PH
        + [pltpu.VMEM((WIN, BLK, HD), bf16)] * PH
        + [pltpu.VMEM((WIN + 1, BLK, HD), bf16)] * PH
        + [pltpu.VMEM((SB // 2, BLK, HD), bf16)] * (3 * PH)
        + [
            pltpu.VMEM((2, BLK, HD), bf16),
            pltpu.VMEM((PH, SB, BLK, HD), bf16),
            pltpu.VMEM((2 * SB, LANES), jnp.int32),
            pltpu.SMEM((SB, LANES), jnp.int32),
        ]
        + [pltpu.VMEM((KB // 2, BLK, 2 * BLK), jnp.float32)] * UNROLL
        + [dma, dma, dma, dma]
        + [dma((PH, 4)), dma((PH, 4)), dma((PH, 4)), dma((2,)), dma]
        + [dma((PH, 2)), dma((PH, 2)), dma((PH, 2))]
        + [dma((PH,)), dma((PH,)), dma((PH,)), dma((PH, 2)), dma((PH, 2)), dma, dma],
        compiler_params=pltpu.CompilerParams(
            collective_id=0, has_side_effects=True, vmem_limit_bytes=48 << 20
        ),
    )(queries, keys, values, lists)


def solution(mesh):
    in_specs = (
        P(("seq", "head"), None),
        P(("seq", "head"), None),
        P(("seq", "head"), None),
        P("seq", None),
        P("seq"),
    )
    out_specs = P(("seq", "head"), None)
    return jax.shard_map(local, mesh=mesh, in_specs=in_specs, out_specs=out_specs, check_vma=False)
```

```python
import functools
import math

import jax
import jax.numpy as jnp
from jax import lax
from jax.experimental import pallas as pl
from jax.experimental.pallas import tpu as pltpu
from jax.sharding import PartitionSpec as P

HD = 128
BLK = 128
KB = 20
SB = 16
HALO = 12
WIN = HALO + SB + HALO
PH = 3
UNROLL = 4
LANES = 128
MESH = pl.DeviceIdType.MESH
EXP2_SCALE = math.log2(math.e) / math.sqrt(HD)


def xor_bit(a, b):
    return a + b - 2 * a * b


def device_at(x, y, z, core):
    return (z // 2) * 8 + y * 2 + core, (z % 2) * 4 + x


def attend(block, q_ref, k_ref, v_ref, ones_ref, lists, s_ref):
    query = q_ref[block]
    top = None
    for c in range(KB // 2):
        picked = [k_ref[lists[block, 2 * c + t]] for t in range(2)]
        scores = lax.dot_general(
            query, jnp.concatenate(picked, axis=0), (((1,), (1,)), ((), ())),
            preferred_element_type=jnp.float32,
        )
        s_ref[c] = scores
        top = scores if top is None else jnp.maximum(top, scores)
    top = jnp.max(top, axis=1, keepdims=True) * EXP2_SCALE
    total = None
    for c in range(KB // 2):
        weights = jnp.exp2(s_ref[c] * EXP2_SCALE - top).astype(jnp.bfloat16)
        picked = [
            jnp.concatenate(
                [v_ref[lists[block, 32 + 2 * c + t]], ones_ref[lists[block, 64 + 2 * c + t]]], axis=1
            )
            for t in range(2)
        ]
        part = jnp.dot(weights, jnp.concatenate(picked, axis=0), preferred_element_type=jnp.float32)
        total = part if total is None else total + part
    return (total[:, :HD] / total[:, HD:]).astype(jnp.bfloat16)


def kernel(*refs):
    q_in, k_in, v_in, listed_in, live_in, out = refs[:6]
    q, k, v = refs[6:9], refs[9:12], refs[12:15]
    q_pass, k_pass, v_pass = refs[15:18], refs[18:21], refs[21:24]
    ones_ref, staged, lists_v, lists_s, listed, live, own_lists = refs[24:31]
    scores = refs[31 : 31 + UNROLL]
    (q_send, k_send, v_send, l_send, q_recv, k_recv, v_recv, l_recv, l_sem,
     qp_recv, kp_recv, vp_recv, qf_send, kf_send, vf_send, kf_recv, vf_recv,
     o_send, o_recv, in_sem) = refs[31 + UNROLL :]

    seq, head = lax.axis_index("seq"), lax.axis_index("head")
    planes = lax.axis_size("seq") // 4
    bands = lax.axis_size("seq") // 2
    y, core, z_lo, x = (seq // 2) % 4, seq % 2, head // 4, head % 4
    z = (seq // 8) * 2 + z_lo
    my_band = 2 * z + core
    my_slot = y * 4 + x
    native = y // 2 == z_lo
    own_core = y % 2
    on_core = own_core == core

    sibling = device_at(x, y, z, 1 - core)
    partner = device_at(x, y, z + 1 - 2 * z_lo, core)
    across = device_at(x, y, (z + 2 * core - 1 + planes) % planes, 1 - core)

    inputs = (
        pltpu.make_async_copy(listed_in, listed, in_sem.at[0]),
        pltpu.make_async_copy(live_in, live, in_sem.at[1]),
    )
    for copy in inputs:
        copy.start()
    ones_ref[0] = jnp.ones((BLK, HD), jnp.bfloat16)
    ones_ref[1] = jnp.zeros((BLK, HD), jnp.bfloat16)
    for h in range(PH):
        v[h][WIN] = jnp.zeros((BLK, HD), jnp.bfloat16)

    bits = [x % 2, x // 2, y % 2, y // 2]

    def slot_at(step):
        flipped = [1 - bit if step >> b & 1 else bit for b, bit in enumerate(bits)]
        return flipped[0] + 2 * flipped[1], flipped[2] + 2 * flipped[3]

    barrier = pltpu.get_barrier_semaphore()

    def greet(device):
        pl.semaphore_signal(barrier, inc=1, device_id=device, device_id_type=MESH)

    def not_me(device):
        return jnp.logical_or(device[0] != seq, device[1] != head)

    for device in (sibling, partner, across):
        greet(device)
    for n in range(SB):
        for device in (
            device_at(n % 4, n // 4, z, own_core),
            device_at(n % 4, core + 2 * (n // 8), z, (n // 4) % 2),
        ):
            pl.when(not_me(device))(functools.partial(greet, device))
    for n in range(SB // 2):
        greet((2 * my_band + n // 4, (1 - z_lo) * 4 + n % 4))

    @pl.when(jnp.logical_not(native))
    def _():
        for n in range(SB):
            greet(device_at(n % 4, n // 4, z + 1 - 2 * z_lo, own_core))

    off_plane, off_core = xor_bit(y // 2, z_lo), xor_bit(own_core, core)
    pl.semaphore_wait(barrier, 2 * SB + SB // 2 + 1 + SB * off_plane + 2 * off_core)

    def start(src, dst, send, recv, device):
        pltpu.make_async_remote_copy(
            src_ref=src, dst_ref=dst, send_sem=send, recv_sem=recv,
            device_id=device, device_id_type=MESH,
        ).start()

    def push(src, dst, send, recv, device):
        @pl.when(not_me(device))
        def _():
            start(src, dst, send, recv, device)

        @pl.when(jnp.logical_not(not_me(device)))
        def _():
            pltpu.make_async_copy(src, dst, recv).start()

    def columns(slot, h):
        return pl.ds(pl.multiple_of((slot * PH + h) * HD, HD), HD)

    def make_lists():
        for copy in inputs:
            copy.wait()
        blocks = bands * SB
        row = lax.broadcasted_iota(jnp.int32, listed.shape, 0)
        counted = sum(jnp.where(row == r, live[r], 0) for r in range(listed.shape[0]))
        counts = lax.broadcasted_iota(jnp.int32, listed.shape, 1) < counted
        own_band = (z // 2) * 4 + y
        window = listed[...] - own_band * SB + HALO
        window = jnp.where(window < 0, window + blocks, window)
        window = jnp.where(window >= blocks, window - blocks, window)
        own_lists[...] = jnp.zeros_like(own_lists)
        own_lists[:, 0:KB] = jnp.where(counts, window, row + (HALO + core * 8))
        own_lists[:, 32 : 32 + KB] = jnp.where(counts, window, WIN)
        own_lists[:, 64 : 64 + KB] = jnp.where(counts, 0, 1)

    def scatter_lists():
        for n in (0, 4, 8, 12):
            tx, ty = slot_at(n)
            push(own_lists, lists_v.at[pl.ds(pl.multiple_of(core * 8, 8), 8)], l_send,
                 l_recv.at[core], device_at(tx, ty, z, own_core))

    def scatter(h):
        def send_all(names):
            @pl.when(native)
            def _():
                for src, dst, _, send, recv, _, first in names:
                    for n in range(SB):
                        tx, ty = slot_at(n)
                        push(src.at[:, columns(ty * 4 + tx, h)],
                             dst[h].at[first + core * 8 + z_lo * 4 + x], send,
                             recv.at[h, core * 2 + z_lo], device_at(tx, ty, z, own_core))

            @pl.when(jnp.logical_not(native))
            def _():
                for src, _, dst, send, _, recv, _ in names:
                    for n in range(SB):
                        tx, ty = slot_at(n)
                        push(src.at[:, columns(ty * 4 + tx, h)],
                             dst[h].at[core * 4 + x], send,
                             recv.at[h, core], device_at(tx, ty, z, own_core))

        send_all(((k_in, k, k_pass, k_send, k_recv, kp_recv, HALO),
                  (v_in, v, v_pass, v_send, v_recv, vp_recv, HALO),
                  (q_in, q, q_pass, q_send, q_recv, qp_recv, 0)))

    def arrived(ref, sem):
        pltpu.make_async_copy(ref, ref, sem).wait()

    def four(start_block):
        return pl.ds(start_block, 4)

    keys = (k, k_pass, kp_recv, kf_send, k_recv, kf_recv)
    values = (v, v_pass, vp_recv, vf_send, v_recv, vf_recv)

    def relay(h, names):
        bufs, passes, pass_recv, send, own_recv, recv = names
        buf, passed = bufs[h], passes[h]
        for part in range(2):
            group, src = part * 2 + z_lo, four(part * 4)
            arrived(passed.at[src], pass_recv.at[h, part])
            start(passed.at[src], buf.at[four(HALO + group * 4)], send.at[h],
                  own_recv.at[h, group], partner)

            @pl.when(jnp.logical_and(core == 1, z_lo == 1))
            def _():
                start(passed.at[src], buf.at[four(part * 8)], send.at[h], recv.at[h, 0], sibling)

            @pl.when(jnp.logical_and(core == 0, z_lo == 0))
            def _():
                start(passed.at[src], buf.at[four(HALO + SB + part * 8)], send.at[h],
                      recv.at[h, 1], sibling)

    def relay_queries(h):
        for part in range(2):
            group, src = part * 2 + z_lo, four(part * 4)
            arrived(q_pass[h].at[src], qp_recv.at[h, part])
            start(q_pass[h].at[src], q[h].at[four(group * 4)], qf_send.at[h],
                  q_recv.at[h, group], partner)

    right = tuple(jnp.where(core == 0, a, b) for a, b in zip(sibling, across))
    left = tuple(jnp.where(core == 0, b, a) for a, b in zip(sibling, across))

    def share(h, which, names):
        bufs, _, _, send, own_recv, recv = names
        buf = bufs[h]
        for part in range(2):
            group = part * 2 + xor_bit(z_lo, which)
            own = four(HALO + group * 4)
            to_right = jnp.logical_and(
                group >= 1,
                jnp.logical_or(jnp.logical_or(core == 0, z_lo == 1), group == 2),
            )
            to_left = jnp.logical_and(
                group <= 2,
                jnp.logical_or(jnp.logical_or(core == 1, z_lo == 0), group == 1),
            )
            arrived(buf.at[own], own_recv.at[h, group])

            @pl.when(to_right)
            def _():
                start(buf.at[own], buf.at[four(group * 4 - 4)], send.at[h], recv.at[h, 0], right)

            @pl.when(to_left)
            def _():
                start(buf.at[own], buf.at[four(HALO + SB + group * 4)], send.at[h],
                      recv.at[h, 1], left)

    def early(h):
        for names in (keys, values):
            relay(h, names)
            share(h, 0, names)

    def late(h, step):
        if step == 0:
            relay_queries(h)
        else:
            share(h, 1, (keys, values)[step - 1])

    scatter(0)
    make_lists()
    pl.when(native)(scatter_lists)
    scatter(1)
    early(0)
    scatter(2)
    for step in range(3):
        late(0, step)
    for band in range(2):
        arrived(lists_v.at[pl.ds(band * 8, 8)], l_recv.at[band])
    move = pltpu.make_async_copy(lists_v.at[pl.ds(0, SB)], lists_s, l_sem)
    move.start()
    move.wait()

    for h in range(PH):
        if h + 1 < PH:
            early(h + 1)
        for group in range(4):
            arrived(q[h].at[four(group * 4)], q_recv.at[h, group])
        for side, first in ((0, 0), (1, HALO + SB)):
            arrived(k[h].at[pl.ds(first, HALO)], kf_recv.at[h, side])
            arrived(v[h].at[pl.ds(first, HALO)], vf_recv.at[h, side])

        @pl.loop(0, SB // UNROLL)
        def _(step):
            if h + 1 < PH:
                for n in range(3):
                    pl.when(step == n)(functools.partial(late, h + 1, n))
            for u in range(UNROLL):
                block = step * UNROLL + u
                staged[h, block] = attend(block, q[h], k[h], v[h], ones_ref, lists_s, scores[u])
            for u in range(UNROLL):
                block = step * UNROLL + u
                push(staged.at[h, block], out.at[:, columns(my_slot, h)], o_send, o_recv,
                     (2 * my_band + block // 8, block % 8))

    arrived(out, o_recv)
    sent = ((k_in, k_send), (v_in, v_send), (q_in, q_send))

    @pl.when(on_core)
    def _():
        for ref, sem in sent:
            arrived(ref.at[:, pl.ds(0, (SB - 1) * PH * HD)], sem)

    @pl.when(jnp.logical_not(on_core))
    def _():
        for ref, sem in sent:
            arrived(ref, sem)

    mine = jnp.logical_and(on_core, native)

    @pl.when(mine)
    def _():
        arrived(staged.at[:, pl.ds(0, SB - 1)], o_send)
        arrived(lists_v.at[pl.ds(0, 24)], l_send)

    @pl.when(jnp.logical_not(mine))
    def _():
        arrived(staged, o_send)

    @pl.when(jnp.logical_and(jnp.logical_not(on_core), native))
    def _():
        arrived(lists_v, l_send)

    @pl.when(core == z_lo)
    def _():
        for h in range(PH):
            arrived(k[h], kf_send.at[h])
            arrived(v[h].at[pl.ds(0, WIN)], vf_send.at[h])

    @pl.when(core != z_lo)
    def _():
        for h in range(PH):
            arrived(k[h].at[pl.ds(0, 2 * HALO)], kf_send.at[h])
            arrived(v[h].at[pl.ds(0, 2 * HALO)], vf_send.at[h])

    for h in range(PH):
        arrived(q_pass[h], qf_send.at[h])


def local(queries, keys, values, block_lists, live_counts):
    hbm = pl.BlockSpec(memory_space=pl.ANY)
    dma = pltpu.SemaphoreType.DMA
    bf16 = jnp.bfloat16
    return pl.pallas_call(
        kernel,
        out_shape=jax.ShapeDtypeStruct(queries.shape, bf16),
        in_specs=[hbm] * 5,
        out_specs=hbm,
        scratch_shapes=[pltpu.VMEM((SB, BLK, HD), bf16)] * PH
        + [pltpu.VMEM((WIN, BLK, HD), bf16)] * PH
        + [pltpu.VMEM((WIN + 1, BLK, HD), bf16)] * PH
        + [pltpu.VMEM((SB // 2, BLK, HD), bf16)] * (3 * PH)
        + [
            pltpu.VMEM((2, BLK, HD), bf16),
            pltpu.VMEM((PH, SB, BLK, HD), bf16),
            pltpu.VMEM((2 * SB, LANES), jnp.int32),
            pltpu.SMEM((SB, LANES), jnp.int32),
            pltpu.VMEM(block_lists.shape, jnp.int32),
            pltpu.SMEM(live_counts.shape, jnp.int32),
            pltpu.VMEM((block_lists.shape[0], LANES), jnp.int32),
        ]
        + [pltpu.VMEM((KB // 2, BLK, 2 * BLK), jnp.float32)] * UNROLL
        + [dma, dma, dma, dma]
        + [dma((PH, 4)), dma((PH, 4)), dma((PH, 4)), dma((2,)), dma]
        + [dma((PH, 2)), dma((PH, 2)), dma((PH, 2))]
        + [dma((PH,)), dma((PH,)), dma((PH,)), dma((PH, 2)), dma((PH, 2)), dma, dma, dma((2,))],
        compiler_params=pltpu.CompilerParams(
            collective_id=0, has_side_effects=True, vmem_limit_bytes=62 << 20
        ),
    )(queries, keys, values, block_lists, live_counts)


def solution(mesh):
    in_specs = (
        P(("seq", "head"), None),
        P(("seq", "head"), None),
        P(("seq", "head"), None),
        P("seq", None),
        P("seq"),
    )
    out_specs = P(("seq", "head"), None)
    return jax.shard_map(local, mesh=mesh, in_specs=in_specs, out_specs=out_specs, check_vma=False)
```
